128 devices in a mesh: src: 16 (over x, z_lo, core), dst: 8 (over z_hi, y).
Axes of the slice: x: 4, y: 4, z: 4 (z_hi: 2, z_lo: 2; z = z_hi * 2 + z_lo), core: 2. Of those that a mesh axis runs over, the one named last changes fastest.
Arguments:
- features: bfloat16 [32768, 1024], P(('src', 'dst')), may hold values from -28 to 28, as said below
- w_src: bfloat16 [1024, 512], replicated, may hold values from -0.1875 to 0.1875
- w_dst: bfloat16 [1024, 512], replicated, may hold values from -0.1875 to 0.1875
- attn: float32 [8, 64], replicated, may hold values from -3 to 3
- bias: float32 [512], replicated, may hold values from -3 to 3
- tile_masks: int32 [16, 8, 16, 8, 128], P('src', 'dst'), may hold values from 0 to 65535, as said below
- tile_dst: int32 [16, 8, 16], P('src', 'dst'), may hold values from 0 to 15, as said below
- tile_src: int32 [16, 8, 16], P('src', 'dst'), may hold values from 0 to 31, as said below
- tile_count: int32 [16, 8], P('src', 'dst'), may hold values from 12 to 16, as said below
Outputs:
- attended: bfloat16 [32768, 512], P(('src', 'dst'))
The draws below stay inside these ranges and needn't reach their ends.
Inputs may be any that keep to these rules, and one draw needn't show every extreme that they name: Every vertex's features lie within the stated range. `tile_masks`: packed edge bits, 16 source columns a word. `tile_dst`: within one grid block the slots name distinct destination tiles. `tile_src`: within one grid block the slots name distinct source tiles. `tile_count`: some grid block uses all 16 slots.
All inputs are finite; a program needn't handle non-finite values.
Results may differ from the reference program's by a relative error of at most 0.0092.
The reference program's roundings to bfloat16 on the way count: a program that leaves them out, or rounds other values in their place, can miss the bound.
Values may be sent and summed in bfloat16 or wider, within the bound.
A program may use at most 64 MiB of HBM per device.

```python
import jax
import jax.numpy as jnp
from jax import lax

V_DEV = 256
F = 1024
H = 8
C = 64
HC = 512
MAXT = 16
N_SRC = 16
N_DST = 8


def draw_tile_dst(key, part):
    key = jax.random.fold_in(key, 3)
    blocks = N_SRC * N_DST
    keys = jax.random.split(key, blocks)

    def choose(single):
        return jax.random.permutation(single, N_DST * V_DEV // 128)[:MAXT]
    picks = jax.vmap(choose)(keys)
    return picks.reshape(N_SRC, N_DST, MAXT).astype(jnp.int32)


def draw_tile_src(key, part):
    key = jax.random.fold_in(key, 4)
    blocks = N_SRC * N_DST
    keys = jax.random.split(key, blocks)

    def choose(single):
        return jax.random.permutation(single, N_SRC * V_DEV // 128)[:MAXT]
    picks = jax.vmap(choose)(keys)
    return picks.reshape(N_SRC, N_DST, MAXT).astype(jnp.int32)


def draw_tile_masks(key, part):
    key = jax.random.fold_in(key, 5)
    first_key, second_key = jax.random.split(key)
    shape = (N_SRC, N_DST, MAXT, 8, 128)
    first = jax.random.randint(first_key, shape, 0, 65536, dtype=jnp.int32)
    second = jax.random.randint(second_key, shape, 0, 65536, dtype=jnp.int32)
    words = first & second
    words = words.at[0, 0, 0, 0, 0].set(jnp.int32(65535))
    words = words.at[0, 0, 0, 1, 0].set(jnp.int32(0))
    return words


def draw_tile_count(key, part):
    key = jax.random.fold_in(key, 7)
    count_key, pick_key = jax.random.split(key)
    counts = jax.random.randint(count_key, (N_SRC * N_DST,), MAXT - MAXT // 4, MAXT + 1, dtype=jnp.int32)
    pick = jax.random.randint(pick_key, (), 0, N_SRC * N_DST, dtype=jnp.int32)
    counts = jnp.where(jnp.arange(N_SRC * N_DST, dtype=jnp.int32) == pick, MAXT, counts)
    return counts.reshape(N_SRC, N_DST).astype(jnp.int32)


def draw_features(key, part):
    key = jax.random.fold_in(key, 11)
    value_key = jax.random.fold_in(key, 0)
    rows = V_DEV * N_SRC * N_DST
    values = jnp.clip(jax.random.normal(value_key, (rows, F), jnp.float32), -6.0, 6.0)
    return values.astype(jnp.bfloat16)


def noise(rng, extent, deviation, reach, held_as=jnp.bfloat16):
    values = deviation * jax.random.normal(rng, extent, jnp.float32)
    return jnp.clip(values, min=-reach, max=reach).astype(held_as)


def setup_inputs(seed: int = 0) -> dict:
    seeds = jax.random.split(jax.random.key(seed), 10)
    features = draw_features(jax.random.fold_in(seeds[9], 71), 0)
    w_src = noise(seeds[1], (F, HC), F ** -0.5, 0.1875)
    w_dst = noise(seeds[2], (F, HC), F ** -0.5, 0.1875)
    attn = noise(seeds[3], (H, C), 0.5, 3.0, jnp.float32)
    bias = noise(seeds[4], (HC,), 0.5, 3.0, jnp.float32)
    tile_masks = draw_tile_masks(jax.random.fold_in(seeds[9], 71), 0)
    tile_dst = draw_tile_dst(jax.random.fold_in(seeds[9], 71), 0)
    tile_src = draw_tile_src(jax.random.fold_in(seeds[9], 71), 0)
    tile_count = draw_tile_count(jax.random.fold_in(seeds[9], 71), 0)
    return dict(features=features, w_src=w_src, w_dst=w_dst, attn=attn, bias=bias, tile_masks=tile_masks, tile_dst=tile_dst, tile_src=tile_src, tile_count=tile_count)


slope = 0.2
floor_value = -1e30


def unpack_edges(words):
    shifts = jnp.arange(16, dtype=jnp.int32)
    bits = (words[:, None, :] >> shifts[None, :, None]) & 1
    return bits.reshape(128, 128).T > 0


def tile_logits(src_tile, dst_tile, attn):
    heads = attn.shape[0]
    left = src_tile.astype(jnp.float32).reshape(128, heads, -1)
    right = dst_tile.astype(jnp.float32).reshape(128, heads, -1)

    def one_head(index):
        src_part = lax.dynamic_index_in_dim(left, index, 1, keepdims=False)
        dst_part = lax.dynamic_index_in_dim(right, index, 1, keepdims=False)
        weight = lax.dynamic_index_in_dim(attn, index, 0, keepdims=False)
        joined = dst_part[:, None, :] + src_part[None, :, :]
        joined = jnp.where(joined > 0, joined, slope * joined)
        return jnp.sum(joined * weight, axis=-1)

    return lax.map(one_head, jnp.arange(heads, dtype=jnp.int32))


def self_logits(own_l, own_r, attn):
    heads = attn.shape[0]
    joined = own_l.astype(jnp.float32).reshape(own_l.shape[0], heads, -1) + own_r.astype(jnp.float32).reshape(own_r.shape[0], heads, -1)
    joined = jnp.where(joined > 0, joined, slope * joined)
    return jnp.sum(joined * attn, axis=-1)


def block_partial(xl_blk, xr_blk, attn, masks, tile_dst, tile_src, count):
    heads = attn.shape[0]
    tiles = masks.shape[0]
    rows = xr_blk.shape[0]
    width = xr_blk.shape[1]

    def first(t, carry):
        logits, best = carry
        src_tile = lax.dynamic_slice_in_dim(xl_blk, tile_src[t] * 128, 128, 0)
        dst_tile = lax.dynamic_slice_in_dim(xr_blk, tile_dst[t] * 128, 128, 0)
        edges = unpack_edges(lax.dynamic_index_in_dim(masks, t, 0, keepdims=False))
        score = jnp.where(edges[None], tile_logits(src_tile, dst_tile, attn), floor_value)
        logits = lax.dynamic_update_index_in_dim(logits, score, t, 0)
        start = tile_dst[t] * 128
        old = lax.dynamic_slice_in_dim(best, start, 128, 0)
        best = lax.dynamic_update_slice_in_dim(best, jnp.maximum(old, jnp.max(score, axis=2).T), start, 0)
        return logits, best

    logits = jnp.full((tiles, heads, 128, 128), floor_value, jnp.float32)
    best = jnp.full((rows, heads), floor_value, jnp.float32)
    logits, best = lax.fori_loop(jnp.int32(0), count, first, (logits, best))

    def second(t, carry):
        total, weight_sum = carry
        start = tile_dst[t] * 128
        edges = unpack_edges(lax.dynamic_index_in_dim(masks, t, 0, keepdims=False))
        top = lax.dynamic_slice_in_dim(best, start, 128, 0).T
        score = lax.dynamic_index_in_dim(logits, t, 0, keepdims=False)
        prob = jnp.where(edges[None], jnp.exp(score - top[:, :, None]), 0.0).astype(jnp.bfloat16)
        src_tile = lax.dynamic_slice_in_dim(xl_blk, tile_src[t] * 128, 128, 0).reshape(128, heads, -1)
        part = jnp.einsum('hds,shc->dhc', prob.astype(jnp.float32), src_tile.astype(jnp.float32)).reshape(128, width)
        old = lax.dynamic_slice_in_dim(total, start, 128, 0)
        total = lax.dynamic_update_slice_in_dim(total, old + part, start, 0)
        old_sum = lax.dynamic_slice_in_dim(weight_sum, start, 128, 0)
        weight_sum = lax.dynamic_update_slice_in_dim(weight_sum, old_sum + jnp.sum(prob.astype(jnp.float32), axis=2).T, start, 0)
        return total, weight_sum

    total = jnp.zeros((rows, width), jnp.float32)
    weight_sum = jnp.zeros((rows, heads), jnp.float32)
    total, weight_sum = lax.fori_loop(jnp.int32(0), count, second, (total, weight_sum))
    return best, total, weight_sum


def combine(self_score, own_l, bests, totals, sums, bias):
    rows, heads = self_score.shape
    top = jnp.maximum(self_score, jnp.max(bests, axis=0))
    scale = jnp.exp(bests - top[None])
    self_weight = jnp.exp(self_score - top)
    values = own_l.astype(jnp.float32).reshape(rows, heads, -1) * self_weight[:, :, None]
    values = values + jnp.sum(totals.reshape(totals.shape[0], rows, heads, -1) * scale[:, :, :, None], axis=0)
    denom = self_weight + jnp.sum(sums * scale, axis=0)
    return ((values / denom[:, :, None]).reshape(rows, -1) + bias).astype(jnp.bfloat16)


def reference(features, w_src, w_dst, attn, bias, tile_masks, tile_dst, tile_src, tile_count):
    xl = jnp.dot(features, w_src, preferred_element_type=jnp.float32).astype(jnp.bfloat16)
    xr = jnp.dot(features, w_dst, preferred_element_type=jnp.float32).astype(jnp.bfloat16)
    width = xl.shape[1]
    grid_l = xl.reshape(N_SRC, N_DST, V_DEV, width)
    grid_r = xr.reshape(N_SRC, N_DST * V_DEV, width)

    def dest_group(s):
        xr_blk = lax.dynamic_index_in_dim(grid_r, s, 0, keepdims=False)
        own_l = lax.dynamic_index_in_dim(grid_l, s, 0, keepdims=False).reshape(N_DST * V_DEV, width)

        def one_block(d):
            xl_blk = lax.dynamic_index_in_dim(grid_l, d, 1, keepdims=False).reshape(N_SRC * V_DEV, width)
            return block_partial(xl_blk, xr_blk, attn, tile_masks[s, d], tile_dst[s, d], tile_src[s, d], tile_count[s, d])

        bests, totals, sums = lax.map(one_block, jnp.arange(N_DST, dtype=jnp.int32))
        self_score = self_logits(own_l, xr_blk, attn)
        return combine(self_score, own_l, bests, totals, sums, bias)

    result = lax.map(dest_group, jnp.arange(N_SRC, dtype=jnp.int32))
    return result.reshape(N_SRC * N_DST * V_DEV, width)
```

```python
import functools

import jax
import jax.numpy as jnp
from jax import lax
from jax.experimental import pallas as pl
from jax.experimental.pallas import tpu as pltpu
from jax.sharding import PartitionSpec as P

f32, bf16, i32 = jnp.float32, jnp.bfloat16, jnp.int32
MESH = pl.DeviceIdType.MESH
TILE = 128
FLOOR = -1e30
HALF_FLOOR = -5e29


def nt(a, b):
    return lax.dot_general(a, b, (((1,), (1,)), ((), ())), preferred_element_type=f32)


def mm(a, b):
    return jnp.dot(a, b, preferred_element_type=f32)


def split(x):
    hi = x.astype(bf16)
    return hi, (x - hi.astype(f32)).astype(bf16)


def iota(shape, dim):
    return lax.broadcasted_iota(i32, shape, dim)


def make_coefficients(attn_ref, alin_ref, aw_ref, brep_ref):
    attn = attn_ref[...]
    tiled = jnp.concatenate([attn] * 8, 1)
    diag = jnp.where(iota((8, 512), 0) == iota((8, 512), 1) // 64, tiled, 0.0)
    flat = jnp.sum(diag, axis=0, keepdims=True)
    same = iota((TILE, TILE), 0) // 64 == iota((TILE, TILE), 1) // 64
    for hp in range(4):
        row = jnp.broadcast_to(flat[:, hp * TILE : (hp + 1) * TILE], (TILE, TILE))
        rep = jnp.where(same, row.T, 0.0)
        parts = split(rep) + split(-0.8 * rep)
        for k, part in enumerate(parts):
            brep_ref[hp, :, k * TILE : (k + 1) * TILE] = part
    k4 = iota((8, TILE), 0) % 4
    half = iota((8, TILE), 1) // 64
    for st in range(2):
        fv = jnp.broadcast_to(flat[:, st * TILE : (st + 1) * TILE], (8, TILE))
        fw = jnp.broadcast_to(flat[:, (st + 2) * TILE : (st + 3) * TILE], (8, TILE))
        lin = jnp.concatenate(
            [jnp.where(k4 == half, fv, 0.0), jnp.where(k4 - 2 == half, fw, 0.0)], 1
        )
        hi, lo = split(lin)
        alin_ref[st] = jnp.concatenate([hi, lo], 0)
        both = -0.8 * jnp.concatenate(
            [jnp.where(k4 == half, fw, 0.0), jnp.where(k4 - 2 == half, fw, 0.0)], 1
        )
        hi, lo = split(both)
        aw_ref[st] = jnp.concatenate([hi, lo], 0)


def prepare_self(st, nu_ref, own_ref, brep_ref, num_ref, den_ref, top_ref):
    for k in range(2):
        ls = slice(k * TILE, (k + 1) * TILE)
        v = own_ref[st, :, ls]
        w = jnp.minimum(nu_ref[st, :, ls].astype(bf16), v)
        b = brep_ref[st + 2 * k]
        top_ref[2 * st + k] = (
            mm(v, b[:, :128]) + mm(v, b[:, 128:256]) + mm(w, b[:, 256:384]) + mm(w, b[:, 384:])
        )
        num_ref[2 * st + k] = v.astype(f32)
        den_ref[2 * st + k] = jnp.ones((256, TILE), f32)


def logits_step(st, dtile, step, nuv_ref, nu_ref, xs_ref, vt_ref, attn_sm, aw_ref, e_ref):
    block = step // 2
    h2 = step % 2
    i0 = pl.multiple_of(dtile * TILE + block * 16, 16)
    ublk = nuv_ref[h2, pl.ds(i0, 16), :]
    i8 = pl.multiple_of(dtile * TILE + block * 16 + h2 * 8, 8)
    rows8 = nu_ref[st, pl.ds(i8, 8), TILE:]
    aw = aw_ref[st]
    low = iota((8, TILE), 0) < 4

    def matrix_piece(quad, g):
        xsw = xs_ref[st, 2 * g + dtile, :, TILE:]
        halves = []
        for a in range(2):
            parts = []
            for b in range(2):
                r = quad * 4 + a * 2 + b
                rb = jnp.broadcast_to(rows8[r : r + 1], (16, TILE)).astype(bf16)
                parts.append(jnp.minimum(jnp.tile(rb, (8, 1)), xsw))
            halves.append(jnp.concatenate(parts, 1))
        res = nt(aw, jnp.concatenate(halves, 0))
        res = res[:8] + res[8:16]
        at = pl.multiple_of(block * 32 + h2 * 16 + quad * 8, 8)
        e_ref[g, 1, pl.ds(at, 8), :] = jnp.where(low, res[:, :TILE], res[:, TILE:])

    pieces = [(q, g) for q in range(2) for g in range(8)]
    done = 0
    acc = [jnp.zeros((16, TILE), f32) for _ in range(8)]
    for c in range(64):
        ub = jnp.broadcast_to(ublk[:, c : c + 1], (16, TILE))
        co = attn_sm[st * 2 + h2, c]
        for g in range(8):
            vb = vt_ref[2 * g + dtile, pl.ds(h2 * 64 + c, 1), :]
            acc[g] = acc[g] + co * jnp.minimum(ub, vb)
        while done < (c + 1) * len(pieces) // 64:
            matrix_piece(*pieces[done])
            done += 1
    for g in range(8):
        e_ref[g, 0, pl.ds(block * 32 + h2, 16, stride=2), :] = -0.8 * acc[g]


def mask_bias(words):
    parts = jnp.concatenate([words & 255, (words >> 8) & 255], 0).astype(f32).astype(bf16)
    k = iota((16, TILE), 0)
    pick = ((k % 8) * 2 + k // 8 == iota((16, TILE), 1) // 8).astype(f32).astype(bf16)
    spread = lax.dot_general(parts, pick, (((0,), (0,)), ((), ())), preferred_element_type=f32)
    bits = spread.astype(i32) & (1 << (iota((TILE, TILE), 1) % 8))
    return jnp.where(bits != 0, 0.0, FLOOR)


def finish_step(st, dtile, step, xs_ref, floor_ref, lin_ref, e_ref, num_ref, den_ref, top_ref):
    g = step // 2
    pair = step % 2
    u = 2 * g + dtile
    even = iota((TILE, TILE), 1) < 64
    evenb = even.astype(f32).astype(bf16)
    oddb = (1 - even.astype(f32)).astype(bf16)
    bias = floor_ref[u]
    ps, ms = [], []
    for h2 in range(2):
        e = e_ref[g, pair, pl.ds(h2, TILE, stride=2), :]
        s = e + (lin_ref[st, u, pl.ds(pair * 2 + h2, 1), :] + bias)
        m = jnp.max(s, axis=1, keepdims=True)
        ps.append(jnp.exp(s - jnp.maximum(m, HALF_FLOOR)).astype(bf16))
        ms.append(m)
    p = jnp.concatenate(ps, 1)
    xp = xs_ref[st, u, :, pl.ds(pl.multiple_of(pair * TILE, TILE), TILE)]
    wt = jnp.concatenate(
        [jnp.concatenate([xp * evenb, evenb], 1), jnp.concatenate([xp * oddb, oddb], 1)], 0
    )
    us = mm(p, wt)
    m = jnp.where(even, ms[0], ms[1])
    at = (2 * st + pair, slice(dtile * TILE, (dtile + 1) * TILE), slice(None))
    old = top_ref[at]
    top = jnp.maximum(old, m)
    a = jnp.exp(old - top)
    b = jnp.exp(m - top)
    top_ref[at] = top
    num_ref[at] = num_ref[at] * a + us[:, :TILE] * b
    den_ref[at] = den_ref[at] * a + us[:, TILE:] * b


def kernel(
    feat_hbm, wsrc_hbm, wdst_hbm, attn_hbm, bias_hbm, mask_hbm, tdst_hbm, tsrc_hbm, count_hbm,
    out_ref,
    feat, wsrc, wdst, attn, bias, mask, attn_sm, tdst, tsrc, tcount, load_sem,
    xg0, xg1, stage, mstage, xs, mk, nu, nuv, own, vt, ea, eb, num, den, top, alin, aw, brep,
    floor_ref, lin, table, gsend, grecv, asend, arecv, msend, mrecv,
):
    s = lax.axis_index("src")
    d = lax.axis_index("dst")
    x, zl, core = s // 4, (s // 2) % 2, s % 2
    zh, y = d // 4, d % 4

    def at(xx, zz, cc):
        return lax.rem(xx + 4, 4) * 4 + zz * 2 + cc

    sib = at(x, zl, 1 - core)
    zn = at(x, 1 - zl, core)
    xp = at(x + 1, zl, core)
    xm = at(x - 1, zl, core)
    dest = [lax.rem(zh + r // 4, 2) * 4 + lax.rem(y + r % 4, 4) for r in range(8)]

    loads = []

    def load(src, dst):
        copy = pltpu.make_async_copy(src, dst, load_sem.at[len(loads)])
        copy.start()
        loads.append(copy)

    def columns(ref, k):
        return ref.at[:, pl.ds(k * TILE, TILE)]

    load(feat_hbm, feat)
    for st in range(2):
        for k in range(2):
            load(columns(wsrc_hbm, st + 2 * k), wsrc.at[st, :, pl.ds(k * TILE, TILE)])
    load(tdst_hbm, tdst)
    load(tsrc_hbm, tsrc)
    load(count_hbm, tcount)
    load(mask_hbm, mask)
    for st in range(2):
        for k in range(2):
            load(columns(wdst_hbm, st + 2 * k), wdst.at[st, :, pl.ds(k * TILE, TILE)])
    load(attn_hbm, attn)
    load(attn_hbm, attn_sm)
    load(bias_hbm, bias)

    barrier = pltpu.get_barrier_semaphore()
    partners = [(p, d) for p in (sib, zn, xp, xm)] + [(s, dest[r]) for r in range(1, 8)]
    for partner in partners:
        pl.semaphore_signal(barrier, inc=1, device_id=partner, device_id_type=MESH)

    xg = (xg0, xg1)
    copies = []

    def send(st, slot, part, to):
        ref = xg[st].at[slot] if part is None else xg[st].at[slot, part]
        copy = pltpu.make_async_remote_copy(
            src_ref=ref,
            dst_ref=ref,
            send_sem=gsend.at[len(copies)],
            recv_sem=grecv.at[st, slot, part or 0],
            device_id=(to, d),
            device_id_type=MESH,
        )
        copy.start()
        copies.append(copy)

    def arrived(st, slot, part=None):
        ref = xg[st].at[slot] if part is None else xg[st].at[slot, part]
        pltpu.make_async_remote_copy(
            src_ref=ref,
            dst_ref=ref,
            send_sem=gsend.at[0],
            recv_sem=grecv.at[st, slot, part or 0],
            device_id=(sib, d),
            device_id_type=MESH,
        ).wait_recv()

    def project(st):
        xl = mm(feat[...], wsrc[st]).astype(bf16)
        own[st] = xl
        xg[st][s] = xl.reshape(2, TILE, 256)

    for copy in loads[:3]:
        copy.wait()
    project(0)
    pl.semaphore_wait(barrier, len(partners))
    for to in (zn, xp, xm, sib):
        send(0, s, None, to)
    for copy in loads[3:5]:
        copy.wait()
    project(1)
    send(1, s, None, zn)

    for copy in loads[5:9]:
        copy.wait()

    def fill(t_dst, _):
        src, slot, used = jnp.int32(0), jnp.int32(0), jnp.int32(0)
        for t in range(16):
            hit = jnp.where((tdst[t] == t_dst) & (t < tcount[0, 0]), 1, 0)
            src, slot, used = src + hit * tsrc[t], slot + hit * t, used + hit
        table[0, t_dst] = src
        table[1, t_dst] = slot
        table[2, t_dst] = used
        return 0

    lax.fori_loop(0, 16, fill, 0)
    mask_copies = []
    for r in range(8):
        for k in range(2):
            tile = dest[r] * 2 + k
            words = mask[table[1, tile]] * table[2, tile]
            if r == 0:
                mk[k] = words
            else:
                mstage[r * 2 + k] = words
        if r:
            copy = pltpu.make_async_remote_copy(
                src_ref=mstage.at[pl.ds(r * 2, 2)],
                dst_ref=mk.at[pl.ds(r * 2, 2)],
                send_sem=msend.at[r],
                recv_sem=mrecv.at[r],
                device_id=(s, dest[r]),
                device_id_type=MESH,
            )
            copy.start()
            mask_copies.append(copy)

    def relay_plane(st):
        arrived(st, zn)
        for to in (xp, xm, sib):
            send(st, zn, None, to)

    def relay_near(st, z):
        left, right = at(x - 1, z, core), at(x + 1, z, core)
        arrived(st, left)
        send(st, left, 0, xp)
        send(st, left, None, sib)
        arrived(st, right)
        send(st, right, 1, xm)
        send(st, right, None, sib)

    def relay_far(st):
        for z in (zl, 1 - zl):
            for part in range(2):
                arrived(st, at(x + 2, z, core), part)
                send(st, at(x + 2, z, core), part, sib)

    def siblings(st):
        for z in (zl, 1 - zl):
            for dx in (0, 1, -1):
                arrived(st, at(x + dx, z, 1 - core))
        for z in (zl, 1 - zl):
            for part in range(2):
                arrived(st, at(x + 2, z, 1 - core), part)

    tile_copies = [[], []]

    def exchange(st):
        for r in (4, 6, 5, 7, 2, 1, 3, 0):
            for k in range(2):
                src = table[0, dest[r] * 2 + k]
                tile = xg[st][src // 2, src % 2]
                if r == 0:
                    xs[st, k] = tile
                else:
                    stage[st, r * 2 + k] = tile
            if r:
                copy = pltpu.make_async_remote_copy(
                    src_ref=stage.at[st, pl.ds(r * 2, 2)],
                    dst_ref=xs.at[st, pl.ds(r * 2, 2)],
                    send_sem=asend.at[st, r],
                    recv_sem=arecv.at[st, r],
                    device_id=(s, dest[r]),
                    device_id_type=MESH,
                )
                copy.start()
                tile_copies[st].append(copy)

    def project_dst(st):
        nu[st] = -mm(feat[...], wdst[st]).astype(bf16).astype(f32)

    relay_plane(0)
    relay_near(0, zl)
    for copy in loads[9:]:
        copy.wait()
    relay_near(0, 1 - zl)
    for to in (xp, xm, sib):
        send(1, s, None, to)
    relay_plane(1)
    project_dst(0)
    relay_far(0)
    siblings(0)
    exchange(0)
    relay_near(1, zl)
    project_dst(1)
    relay_near(1, 1 - zl)
    make_coefficients(attn, alin, aw, brep)
    for st in range(2):
        prepare_self(st, nu, own, brep, num, den, top)
    relay_far(1)
    for copy in mask_copies:
        copy.wait_recv()

    def floors(u, _):
        floor_ref[u] = mask_bias(mk[u])
        return 0

    lax.fori_loop(0, 16, floors, 0)
    siblings(1)
    exchange(1)

    def begin(st):
        for copy in tile_copies[st]:
            copy.wait_recv()
        for h2 in range(2):
            part = nu[st, :, :TILE]
            nuv[h2] = part if h2 == 0 else pltpu.roll(part, 64, 1)

        def turn(u, _):
            vt[u] = xs[st, u, :, :TILE].astype(f32).T
            res = nt(alin[st], xs[st, u])
            lin[st, u] = res[:8] + res[8:]
            return 0

        lax.fori_loop(0, 16, turn, 0, unroll=4)

    def run(now, before):
        def step(n, _):
            if before is not None:
                finish_step(
                    before[0], before[1], n, xs, floor_ref, lin, before[2], num, den, top
                )
            if now is not None:
                logits_step(now[0], now[1], n, nuv, nu, xs, vt, attn_sm, aw, now[2])
            return 0

        lax.fori_loop(0, 16, step, 0)

    phases = [(0, 0, ea), (0, 1, eb), (1, 0, ea), (1, 1, eb)]
    for k, now in enumerate(phases):
        if k % 2 == 0:
            begin(now[0])
        run(now, phases[k - 1] if k else None)
    run(None, phases[-1])

    for st in range(2):
        for k in range(2):
            q = 2 * st + k
            ls = slice((st + 2 * k) * TILE, (st + 2 * k + 1) * TILE)
            out_ref[:, ls] = (num[q] / den[q] + bias[:, ls]).astype(bf16)
    for copy in copies + mask_copies + tile_copies[0] + tile_copies[1]:
        copy.wait_send()


def body(features, w_src, w_dst, attn, bias, tile_masks, tile_dst, tile_src, tile_count):
    hbm = pl.BlockSpec(memory_space=pl.ANY)
    dma = pltpu.SemaphoreType.DMA
    scratch = [
        pltpu.VMEM((256, 1024), bf16),
        pltpu.VMEM((2, 1024, 256), bf16),
        pltpu.VMEM((2, 1024, 256), bf16),
        pltpu.VMEM((8, 64), f32),
        pltpu.VMEM((1, 512), f32),
        pltpu.VMEM((16, 8, TILE), i32),
        pltpu.SMEM((8, 64), f32),
        pltpu.SMEM((16,), i32),
        pltpu.SMEM((16,), i32),
        pltpu.SMEM((1, 1), i32),
        dma((16,)),
        pltpu.VMEM((16, 2, TILE, 256), bf16),
        pltpu.VMEM((16, 2, TILE, 256), bf16),
        pltpu.VMEM((2, 16, TILE, 256), bf16),
        pltpu.VMEM((16, 8, TILE), i32),
        pltpu.VMEM((2, 16, TILE, 256), bf16),
        pltpu.VMEM((16, 8, TILE), i32),
        pltpu.VMEM((2, 256, 256), f32),
        pltpu.VMEM((2, 256, TILE), f32),
        pltpu.VMEM((2, 256, 256), bf16),
        pltpu.VMEM((16, TILE, TILE), f32),
        pltpu.VMEM((8, 2, 256, TILE), f32),
        pltpu.VMEM((8, 2, 256, TILE), f32),
        pltpu.VMEM((4, 256, TILE), f32),
        pltpu.VMEM((4, 256, TILE), f32),
        pltpu.VMEM((4, 256, TILE), f32),
        pltpu.VMEM((2, 16, 256), bf16),
        pltpu.VMEM((2, 16, 256), bf16),
        pltpu.VMEM((4, TILE, 512), bf16),
        pltpu.VMEM((16, TILE, TILE), f32),
        pltpu.VMEM((2, 16, 8, TILE), f32),
        pltpu.SMEM((3, 16), i32),
        dma((38,)),
        dma((2, 16, 2)),
        dma((2, 8)),
        dma((2, 8)),
        dma((8,)),
        dma((8,)),
    ]
    return pl.pallas_call(
        kernel,
        out_shape=jax.ShapeDtypeStruct((256, 512), bf16),
        in_specs=[hbm] * 9,
        out_specs=pl.BlockSpec(memory_space=pltpu.VMEM),
        scratch_shapes=scratch,
        compiler_params=pltpu.CompilerParams(
            collective_id=0, has_side_effects=True, vmem_limit_bytes=60 * 2**20
        ),
    )(
        features, w_src, w_dst, attn, bias.reshape(1, 512), tile_masks[0, 0],
        tile_dst[0, 0], tile_src[0, 0], tile_count,
    )


def solution(mesh):
    return jax.shard_map(
        body,
        mesh=mesh,
        in_specs=(
            P(("src", "dst"), None),
            P(),
            P(),
            P(),
            P(),
            P("src", "dst", None, None, None),
            P("src", "dst", None),
            P("src", "dst", None),
            P("src", "dst"),
        ),
        out_specs=P(("src", "dst"), None),
        check_vma=False,
    )
```

```python
import functools

import jax
import jax.numpy as jnp
from jax import lax
from jax.experimental import pallas as pl
from jax.experimental.pallas import tpu as pltpu
from jax.sharding import PartitionSpec as P

f32, bf16, i32 = jnp.float32, jnp.bfloat16, jnp.int32
MESH = pl.DeviceIdType.MESH
TILE = 128
FLOOR = -1e30
HALF_FLOOR = -5e29


def nt(a, b):
    return lax.dot_general(a, b, (((1,), (1,)), ((), ())), preferred_element_type=f32)


def mm(a, b):
    return jnp.dot(a, b, preferred_element_type=f32)


def split(x):
    hi = x.astype(bf16)
    return hi, (x - hi.astype(f32)).astype(bf16)


def iota(shape, dim):
    return lax.broadcasted_iota(i32, shape, dim)


def make_coefficients(attn_ref, alin_ref, aw_ref, brep_ref):
    attn = attn_ref[...]
    tiled = jnp.concatenate([attn] * 8, 1)
    diag = jnp.where(iota((8, 512), 0) == iota((8, 512), 1) // 64, tiled, 0.0)
    flat = jnp.sum(diag, axis=0, keepdims=True)
    same = iota((TILE, TILE), 0) // 64 == iota((TILE, TILE), 1) // 64
    for hp in range(4):
        row = jnp.broadcast_to(flat[:, hp * TILE : (hp + 1) * TILE], (TILE, TILE))
        rep = jnp.where(same, row.T, 0.0)
        parts = split(rep) + split(-0.8 * rep)
        for k, part in enumerate(parts):
            brep_ref[hp, :, k * TILE : (k + 1) * TILE] = part
    k4 = iota((8, TILE), 0) % 4
    half = iota((8, TILE), 1) // 64
    for st in range(2):
        fv = jnp.broadcast_to(flat[:, st * TILE : (st + 1) * TILE], (8, TILE))
        fw = jnp.broadcast_to(flat[:, (st + 2) * TILE : (st + 3) * TILE], (8, TILE))
        lin = jnp.concatenate(
            [jnp.where(k4 == half, fv, 0.0), jnp.where(k4 - 2 == half, fw, 0.0)], 1
        )
        hi, lo = split(lin)
        alin_ref[st] = jnp.concatenate([hi, lo], 0)
        both = -0.8 * jnp.concatenate(
            [jnp.where(k4 == half, fw, 0.0), jnp.where(k4 - 2 == half, fw, 0.0)], 1
        )
        hi, lo = split(both)
        aw_ref[st] = jnp.concatenate([hi, lo], 0)


def prepare_self(st, nu_ref, own_ref, brep_ref, num_ref, den_ref, top_ref):
    for k in range(2):
        ls = slice(k * TILE, (k + 1) * TILE)
        v = own_ref[st, :, ls]
        w = jnp.minimum(nu_ref[st, :, ls].astype(bf16), v)
        b = brep_ref[st + 2 * k]
        top_ref[2 * st + k] = (
            mm(v, b[:, :128]) + mm(v, b[:, 128:256]) + mm(w, b[:, 256:384]) + mm(w, b[:, 384:])
        )
        num_ref[2 * st + k] = v.astype(f32)
        den_ref[2 * st + k] = jnp.ones((256, TILE), f32)


def logits_step(st, dtile, step, nuv_ref, nu_ref, xs_ref, vt_ref, attn_sm, aw_ref, e_ref):
    block = step // 2
    h2 = step % 2
    i0 = pl.multiple_of(dtile * TILE + block * 16, 16)
    ublk = nuv_ref[h2, pl.ds(i0, 16), :]
    i8 = pl.multiple_of(dtile * TILE + block * 16 + h2 * 8, 8)
    rows8 = nu_ref[st, pl.ds(i8, 8), TILE:]
    aw = aw_ref[st]
    low = iota((8, TILE), 0) < 4

    def matrix_piece(quad, g):
        xsw = xs_ref[st, 2 * g + dtile, :, TILE:]
        halves = []
        for a in range(2):
            parts = []
            for b in range(2):
                r = quad * 4 + a * 2 + b
                rb = jnp.broadcast_to(rows8[r : r + 1], (16, TILE)).astype(bf16)
                parts.append(jnp.minimum(jnp.tile(rb, (8, 1)), xsw))
            halves.append(jnp.concatenate(parts, 1))
        res = nt(aw, jnp.concatenate(halves, 0))
        res = res[:8] + res[8:16]
        at = pl.multiple_of(block * 32 + h2 * 16 + quad * 8, 8)
        e_ref[g, 1, pl.ds(at, 8), :] = jnp.where(low, res[:, :TILE], res[:, TILE:])
        tokens.append(res[:, :TILE] * 0.0)

    pieces = [(q, g) for q in range(2) for g in range(8)]
    done = 0
    tokens = []
    acc = [jnp.zeros((16, TILE), f32) for _ in range(8)]
    for c in range(64):
        ub = jnp.broadcast_to(ublk[:, c : c + 1], (16, TILE))
        k = c // 4 - 2
        if c % 4 == 0 and 0 <= k < len(tokens):
            ub = ub + jnp.concatenate([tokens[k]] * 2, 0)
        co = attn_sm[st * 2 + h2, c]
        for g in range(8):
            vb = vt_ref[2 * g + dtile, pl.ds(h2 * 64 + c, 1), :]
            acc[g] = acc[g] + co * jnp.minimum(ub, vb)
        while done < len(pieces) and c >= 4 * done - 12:
            matrix_piece(*pieces[done])
            done += 1
    for g in range(8):
        e_ref[g, 0, pl.ds(block * 32 + h2, 16, stride=2), :] = -0.8 * acc[g]


def mask_bias(words):
    parts = jnp.concatenate([words & 255, (words >> 8) & 255], 0).astype(f32).astype(bf16)
    k = iota((16, TILE), 0)
    pick = ((k % 8) * 2 + k // 8 == iota((16, TILE), 1) // 8).astype(f32).astype(bf16)
    spread = lax.dot_general(parts, pick, (((0,), (0,)), ((), ())), preferred_element_type=f32)
    bits = spread.astype(i32) & (1 << (iota((TILE, TILE), 1) % 8))
    return jnp.where(bits != 0, 0.0, FLOOR)


def finish_step(st, dtile, step, xs_ref, floor_ref, lin_ref, e_ref, num_ref, den_ref, top_ref):
    g = step // 2
    pair = step % 2
    u = 2 * g + dtile
    even = iota((TILE, TILE), 1) < 64
    evenb = even.astype(f32).astype(bf16)
    oddb = (1 - even.astype(f32)).astype(bf16)
    bias = floor_ref[u]
    ps, ms = [], []
    for h2 in range(2):
        e = e_ref[g, pair, pl.ds(h2, TILE, stride=2), :]
        s = e + (lin_ref[st, u, pl.ds(pair * 2 + h2, 1), :] + bias)
        m = jnp.max(s, axis=1, keepdims=True)
        ps.append(jnp.exp(s - jnp.maximum(m, HALF_FLOOR)).astype(bf16))
        ms.append(m)
    p = jnp.concatenate(ps, 1)
    xp = xs_ref[st, u, :, pl.ds(pl.multiple_of(pair * TILE, TILE), TILE)]
    wt = jnp.concatenate(
        [jnp.concatenate([xp * evenb, evenb], 1), jnp.concatenate([xp * oddb, oddb], 1)], 0
    )
    us = mm(p, wt)
    m = jnp.where(even, ms[0], ms[1])
    at = (2 * st + pair, pl.ds(pl.multiple_of(dtile * TILE, TILE), TILE), slice(None))
    old = top_ref[at]
    top = jnp.maximum(old, m)
    a = jnp.exp(old - top)
    b = jnp.exp(m - top)
    top_ref[at] = top
    num_ref[at] = num_ref[at] * a + us[:, :TILE] * b
    den_ref[at] = den_ref[at] * a + us[:, TILE:] * b


def kernel(
    feat_hbm, wsrc_hbm, wdst_hbm, attn_hbm, bias_hbm, mask_hbm, tdst_hbm, tsrc_hbm, count_hbm,
    out_ref,
    feat, wsrc, wdst, attn, bias, mask, attn_sm, tdst, tsrc, tcount, load_sem,
    xg0, xg1, stage, mstage, xs, mk, nu, nuv, own, vt, e_ref, num, den, top, alin, aw, brep,
    floor_ref, lin, table, gsend, grecv, asend, arecv, msend, mrecv,
):
    s = lax.axis_index("src")
    d = lax.axis_index("dst")
    x, zl, core = s // 4, (s // 2) % 2, s % 2
    zh, y = d // 4, d % 4

    def at(xx, zz, cc):
        return lax.rem(xx + 4, 4) * 4 + zz * 2 + cc

    sib = at(x, zl, 1 - core)
    zn = at(x, 1 - zl, core)
    xp = at(x + 1, zl, core)
    xm = at(x - 1, zl, core)
    dest = [lax.rem(zh + r // 4, 2) * 4 + lax.rem(y + r % 4, 4) for r in range(8)]

    loads = []

    def load(src, dst):
        copy = pltpu.make_async_copy(src, dst, load_sem.at[len(loads)])
        copy.start()
        loads.append(copy)

    def columns(ref, k):
        return ref.at[:, pl.ds(k * TILE, TILE)]

    load(feat_hbm, feat)
    for st in range(2):
        for k in range(2):
            load(columns(wsrc_hbm, st + 2 * k), wsrc.at[st, :, pl.ds(k * TILE, TILE)])
    load(tdst_hbm, tdst)
    load(tsrc_hbm, tsrc)
    load(count_hbm, tcount)
    load(mask_hbm, mask)
    for st in range(2):
        for k in range(2):
            load(columns(wdst_hbm, st + 2 * k), wdst.at[st, :, pl.ds(k * TILE, TILE)])
    load(attn_hbm, attn)
    load(attn_hbm, attn_sm)
    load(bias_hbm, bias)

    barrier = pltpu.get_barrier_semaphore()
    partners = [(p, d) for p in (sib, zn, xp, xm)] + [(s, dest[r]) for r in range(1, 8)]
    for partner in partners:
        pl.semaphore_signal(barrier, inc=1, device_id=partner, device_id_type=MESH)

    xg = (xg0, xg1)
    copies = []

    def send(st, slot, part, to):
        ref = xg[st].at[slot] if part is None else xg[st].at[slot, part]
        copy = pltpu.make_async_remote_copy(
            src_ref=ref,
            dst_ref=ref,
            send_sem=gsend.at[len(copies)],
            recv_sem=grecv.at[st, slot, part or 0],
            device_id=(to, d),
            device_id_type=MESH,
        )
        copy.start()
        copies.append(copy)

    def arrived(st, slot, part=None):
        ref = xg[st].at[slot] if part is None else xg[st].at[slot, part]
        pltpu.make_async_remote_copy(
            src_ref=ref,
            dst_ref=ref,
            send_sem=gsend.at[0],
            recv_sem=grecv.at[st, slot, part or 0],
            device_id=(sib, d),
            device_id_type=MESH,
        ).wait_recv()

    def project(st):
        xl = mm(feat[...], wsrc[st]).astype(bf16)
        own[st] = xl
        xg[st][s] = xl.reshape(2, TILE, 256)

    for copy in loads[:3]:
        copy.wait()
    project(0)
    pl.semaphore_wait(barrier, len(partners))
    for to in (zn, xp, xm, sib):
        send(0, s, None, to)
    for copy in loads[3:5]:
        copy.wait()
    project(1)
    send(1, s, None, zn)

    def relay_plane(st):
        arrived(st, zn)
        for to in (xp, xm, sib):
            send(st, zn, None, to)

    def relay_near(st, z):
        left, right = at(x - 1, z, core), at(x + 1, z, core)
        arrived(st, left)
        send(st, left, 0, xp)
        send(st, left, None, sib)
        arrived(st, right)
        send(st, right, 1, xm)
        send(st, right, None, sib)

    def relay_far(st):
        for z in (zl, 1 - zl):
            for part in range(2):
                arrived(st, at(x + 2, z, core), part)
                send(st, at(x + 2, z, core), part, sib)

    def siblings(st):
        for z in (zl, 1 - zl):
            for dx in (0, 1, -1):
                arrived(st, at(x + dx, z, 1 - core))
        for z in (zl, 1 - zl):
            for part in range(2):
                arrived(st, at(x + 2, z, 1 - core), part)

    tile_copies = {}

    def exchange(st):
        for k in range(2):
            for r in (4, 6, 5, 7, 2, 1, 3, 0):
                src = table[0, dest[r] * 2 + k]
                tile = xg[st][src // 2, src % 2]
                if r == 0:
                    xs[st, k] = tile
                    continue
                stage[st, r * 2 + k] = tile
                copy = pltpu.make_async_remote_copy(
                    src_ref=stage.at[st, r * 2 + k],
                    dst_ref=xs.at[st, r * 2 + k],
                    send_sem=asend.at[st, k, r],
                    recv_sem=arecv.at[st, k, r],
                    device_id=(s, dest[r]),
                    device_id_type=MESH,
                )
                copy.start()
                tile_copies[st, k, r] = copy

    def project_dst(st):
        nu[st] = -mm(feat[...], wdst[st]).astype(bf16).astype(f32)

    relay_plane(0)
    relay_near(0, zl)
    for copy in loads[9:]:
        copy.wait()
    relay_near(0, 1 - zl)
    for to in (xp, xm, sib):
        send(1, s, None, to)
    relay_plane(1)

    for copy in loads[5:9]:
        copy.wait()

    def fill(t_dst, _):
        src, slot, used = jnp.int32(0), jnp.int32(0), jnp.int32(0)
        for t in range(16):
            hit = jnp.where((tdst[t] == t_dst) & (t < tcount[0, 0]), 1, 0)
            src, slot, used = src + hit * tsrc[t], slot + hit * t, used + hit
        table[0, t_dst] = src
        table[1, t_dst] = slot
        table[2, t_dst] = used
        return 0

    lax.fori_loop(0, 16, fill, 0)
    mask_copies = []
    for r in range(8):
        for k in range(2):
            tile = dest[r] * 2 + k
            words = mask[table[1, tile]] * table[2, tile]
            if r == 0:
                mk[k] = words
            else:
                mstage[r * 2 + k] = words
        if r:
            copy = pltpu.make_async_remote_copy(
                src_ref=mstage.at[pl.ds(r * 2, 2)],
                dst_ref=mk.at[pl.ds(r * 2, 2)],
                send_sem=msend.at[r],
                recv_sem=mrecv.at[r],
                device_id=(s, dest[r]),
                device_id_type=MESH,
            )
            copy.start()
            mask_copies.append(copy)

    relay_far(0)
    siblings(0)
    exchange(0)
    project_dst(0)
    relay_near(1, zl)
    project_dst(1)
    relay_near(1, 1 - zl)
    make_coefficients(attn, alin, aw, brep)
    for st in range(2):
        prepare_self(st, nu, own, brep, num, den, top)
    for copy in mask_copies:
        copy.wait_recv()

    def floors(u, _):
        floor_ref[u] = mask_bias(mk[u])
        return 0

    lax.fori_loop(0, 16, floors, 0, unroll=2)
    relay_far(1)

    def begin(st, dtile):
        for r in range(1, 8):
            tile_copies[st, dtile, r].wait_recv()
        if dtile == 0:
            for h2 in range(2):
                part = nu[st, :, :TILE]
                nuv[h2] = part if h2 == 0 else pltpu.roll(part, 64, 1)

        def turn(g, _):
            u = 2 * g + dtile
            vt[u] = xs[st, u, :, :TILE].astype(f32).T
            res = nt(alin[st], xs[st, u])
            lin[st, u] = res[:8] + res[8:]
            return 0

        lax.fori_loop(0, 8, turn, 0, unroll=4)

    for st in range(2):
        for dtile in range(2):
            if (st, dtile) == (0, 1):
                siblings(1)
                exchange(1)
            begin(st, dtile)

            def step(n, _):
                logits_step(st, dtile, n, nuv, nu, xs, vt, attn_sm, aw, e_ref)
                return 0

            def finish(n, _):
                finish_step(st, dtile, n, xs, floor_ref, lin, e_ref, num, den, top)
                return 0

            lax.fori_loop(0, 16, step, 0, unroll=2)
            lax.fori_loop(0, 16, finish, 0, unroll=4)

    for st in range(2):
        for k in range(2):
            q = 2 * st + k
            ls = slice((st + 2 * k) * TILE, (st + 2 * k + 1) * TILE)
            out_ref[:, ls] = (num[q] / den[q] + bias[:, ls]).astype(bf16)
    for copy in copies + mask_copies + list(tile_copies.values()):
        copy.wait_send()


def body(features, w_src, w_dst, attn, bias, tile_masks, tile_dst, tile_src, tile_count):
    hbm = pl.BlockSpec(memory_space=pl.ANY)
    dma = pltpu.SemaphoreType.DMA
    scratch = [
        pltpu.VMEM((256, 1024), bf16),
        pltpu.VMEM((2, 1024, 256), bf16),
        pltpu.VMEM((2, 1024, 256), bf16),
        pltpu.VMEM((8, 64), f32),
        pltpu.VMEM((1, 512), f32),
        pltpu.VMEM((16, 8, TILE), i32),
        pltpu.SMEM((8, 64), f32),
        pltpu.SMEM((16,), i32),
        pltpu.SMEM((16,), i32),
        pltpu.SMEM((1, 1), i32),
        dma((16,)),
        pltpu.VMEM((16, 2, TILE, 256), bf16),
        pltpu.VMEM((16, 2, TILE, 256), bf16),
        pltpu.VMEM((2, 16, TILE, 256), bf16),
        pltpu.VMEM((16, 8, TILE), i32),
        pltpu.VMEM((2, 16, TILE, 256), bf16),
        pltpu.VMEM((16, 8, TILE), i32),
        pltpu.VMEM((2, 256, 256), f32),
        pltpu.VMEM((2, 256, TILE), f32),
        pltpu.VMEM((2, 256, 256), bf16),
        pltpu.VMEM((16, TILE, TILE), f32),
        pltpu.VMEM((8, 2, 256, TILE), f32),
        pltpu.VMEM((4, 256, TILE), f32),
        pltpu.VMEM((4, 256, TILE), f32),
        pltpu.VMEM((4, 256, TILE), f32),
        pltpu.VMEM((2, 16, 256), bf16),
        pltpu.VMEM((2, 16, 256), bf16),
        pltpu.VMEM((4, TILE, 512), bf16),
        pltpu.VMEM((16, TILE, TILE), f32),
        pltpu.VMEM((2, 16, 8, TILE), f32),
        pltpu.SMEM((3, 16), i32),
        dma((38,)),
        dma((2, 16, 2)),
        dma((2, 2, 8)),
        dma((2, 2, 8)),
        dma((8,)),
        dma((8,)),
    ]
    return pl.pallas_call(
        kernel,
        out_shape=jax.ShapeDtypeStruct((256, 512), bf16),
        in_specs=[hbm] * 9,
        out_specs=pl.BlockSpec(memory_space=pltpu.VMEM),
        scratch_shapes=scratch,
        compiler_params=pltpu.CompilerParams(
            collective_id=0, has_side_effects=True, vmem_limit_bytes=60 * 2**20
        ),
    )(
        features, w_src, w_dst, attn, bias.reshape(1, 512), tile_masks[0, 0],
        tile_dst[0, 0], tile_src[0, 0], tile_count,
    )


def solution(mesh):
    return jax.shard_map(
        body,
        mesh=mesh,
        in_specs=(
            P(("src", "dst"), None),
            P(),
            P(),
            P(),
            P(),
            P("src", "dst", None, None, None),
            P("src", "dst", None),
            P("src", "dst", None),
            P("src", "dst"),
        ),
        out_specs=P(("src", "dst"), None),
        check_vma=False,
    )
```

```python
import functools

import jax
import jax.numpy as jnp
from jax import lax
from jax.experimental import pallas as pl
from jax.experimental.pallas import tpu as pltpu
from jax.sharding import PartitionSpec as P

f32, bf16, i32 = jnp.float32, jnp.bfloat16, jnp.int32
MESH = pl.DeviceIdType.MESH
TILE = 128
FLOOR = -1e30
HALF_FLOOR = -5e29


def nt(a, b):
    return lax.dot_general(a, b, (((1,), (1,)), ((), ())), preferred_element_type=f32)


def mm(a, b):
    return jnp.dot(a, b, preferred_element_type=f32)


def split(x):
    hi = x.astype(bf16)
    return hi, (x - hi.astype(f32)).astype(bf16)


def iota(shape, dim):
    return lax.broadcasted_iota(i32, shape, dim)


def make_coefficients(attn_ref, alin_ref, aw_ref, brep_ref):
    attn = attn_ref[...]
    tiled = jnp.concatenate([attn] * 8, 1)
    diag = jnp.where(iota((8, 512), 0) == iota((8, 512), 1) // 64, tiled, 0.0)
    flat = jnp.sum(diag, axis=0, keepdims=True)
    same = iota((TILE, TILE), 0) // 64 == iota((TILE, TILE), 1) // 64
    for hp in range(4):
        row = jnp.broadcast_to(flat[:, hp * TILE : (hp + 1) * TILE], (TILE, TILE))
        rep = jnp.where(same, row.T, 0.0)
        parts = split(rep) + split(-0.8 * rep)
        for k, part in enumerate(parts):
            brep_ref[hp, :, k * TILE : (k + 1) * TILE] = part
    k4 = iota((8, TILE), 0) % 4
    half = iota((8, TILE), 1) // 64
    for st in range(2):
        fv = jnp.broadcast_to(flat[:, st * TILE : (st + 1) * TILE], (8, TILE))
        fw = jnp.broadcast_to(flat[:, (st + 2) * TILE : (st + 3) * TILE], (8, TILE))
        lin = jnp.concatenate(
            [jnp.where(k4 == half, fv, 0.0), jnp.where(k4 - 2 == half, fw, 0.0)], 1
        )
        hi, lo = split(lin)
        alin_ref[st] = jnp.concatenate([hi, lo], 0)
        both = -0.8 * jnp.concatenate(
            [jnp.where(k4 == half, fw, 0.0), jnp.where(k4 - 2 == half, fw, 0.0)], 1
        )
        hi, lo = split(both)
        aw_ref[st] = jnp.concatenate([hi, lo], 0)


def prepare_self(st, nu_ref, own_ref, brep_ref, num_ref, den_ref, top_ref):
    for k in range(2):
        ls = slice(k * TILE, (k + 1) * TILE)
        v = own_ref[st, :, ls]
        w = jnp.minimum(nu_ref[st, :, ls].astype(bf16), v)
        b = brep_ref[st + 2 * k]
        top_ref[2 * st + k] = (
            mm(v, b[:, :128]) + mm(v, b[:, 128:256]) + mm(w, b[:, 256:384]) + mm(w, b[:, 384:])
        )
        num_ref[2 * st + k] = v.astype(f32)
        den_ref[2 * st + k] = jnp.ones((256, TILE), f32)


def logits_step(st, dtile, step, nuv_ref, nu_ref, xs_ref, vt_ref, attn_sm, aw_ref, e_ref):
    block = step // 2
    h2 = step % 2
    i0 = pl.multiple_of(dtile * TILE + block * 16, 16)
    ublk = nuv_ref[h2, pl.ds(i0, 16), :]
    i8 = pl.multiple_of(dtile * TILE + block * 16 + h2 * 8, 8)
    rows8 = nu_ref[st, pl.ds(i8, 8), TILE:]
    aw = aw_ref[st]
    low = iota((8, TILE), 0) < 4

    def matrix_piece(quad, g):
        xsw = xs_ref[st, 2 * g + dtile, :, TILE:]
        halves = []
        for a in range(2):
            parts = []
            for b in range(2):
                r = quad * 4 + a * 2 + b
                rb = jnp.broadcast_to(rows8[r : r + 1], (16, TILE)).astype(bf16)
                parts.append(jnp.minimum(jnp.tile(rb, (8, 1)), xsw))
            halves.append(jnp.concatenate(parts, 1))
        res = nt(aw, jnp.concatenate(halves, 0))
        res = res[:8] + res[8:16]
        at = pl.multiple_of(block * 32 + h2 * 16 + quad * 8, 8)
        e_ref[g, 1, pl.ds(at, 8), :] = jnp.where(low, res[:, :TILE], res[:, TILE:])
        tokens.append(res[:, :TILE] * 0.0)

    pieces = [(q, g) for q in range(2) for g in range(8)]
    done = 0
    tokens = []
    acc = [jnp.zeros((16, TILE), f32) for _ in range(8)]
    for c in range(64):
        ub = jnp.broadcast_to(ublk[:, c : c + 1], (16, TILE))
        k = c // 4 - 1
        if c % 4 == 0 and 0 <= k < len(tokens):
            ub = ub + jnp.concatenate([tokens[k]] * 2, 0)
        co = attn_sm[st * 2 + h2, c]
        for g in range(8):
            vb = vt_ref[2 * g + dtile, pl.ds(h2 * 64 + c, 1), :]
            acc[g] = acc[g] + co * jnp.minimum(ub, vb)
        while done < len(pieces) and c >= 4 * done - 12:
            matrix_piece(*pieces[done])
            done += 1
    for g in range(8):
        e_ref[g, 0, pl.ds(block * 32 + h2, 16, stride=2), :] = -0.8 * acc[g]


def mask_bias(words):
    parts = jnp.concatenate([words & 255, (words >> 8) & 255], 0).astype(f32).astype(bf16)
    k = iota((16, TILE), 0)
    pick = ((k % 8) * 2 + k // 8 == iota((16, TILE), 1) // 8).astype(f32).astype(bf16)
    spread = lax.dot_general(parts, pick, (((0,), (0,)), ((), ())), preferred_element_type=f32)
    bits = spread.astype(i32) & (1 << (iota((TILE, TILE), 1) % 8))
    return jnp.where(bits != 0, 0.0, FLOOR)


def finish_step(st, dtile, step, xs_ref, floor_ref, lin_ref, e_ref, num_ref, den_ref, top_ref):
    g = step // 2
    pair = step % 2
    u = 2 * g + dtile
    even = iota((TILE, TILE), 1) < 64
    evenb = even.astype(f32).astype(bf16)
    oddb = (1 - even.astype(f32)).astype(bf16)
    bias = floor_ref[u]
    ps, ms = [], []
    for h2 in range(2):
        e = e_ref[g, pair, pl.ds(h2, TILE, stride=2), :]
        s = e + (lin_ref[st, u, pl.ds(pair * 2 + h2, 1), :] + bias)
        m = jnp.max(s, axis=1, keepdims=True)
        ps.append(jnp.exp(s - jnp.maximum(m, HALF_FLOOR)).astype(bf16))
        ms.append(m)
    p = jnp.concatenate(ps, 1)
    xp = xs_ref[st, u, :, pl.ds(pl.multiple_of(pair * TILE, TILE), TILE)]
    wt = jnp.concatenate(
        [jnp.concatenate([xp * evenb, evenb], 1), jnp.concatenate([xp * oddb, oddb], 1)], 0
    )
    us = mm(p, wt)
    m = jnp.where(even, ms[0], ms[1])
    at = (2 * st + pair, pl.ds(pl.multiple_of(dtile * TILE, TILE), TILE), slice(None))
    old = top_ref[at]
    top = jnp.maximum(old, m)
    a = jnp.exp(old - top)
    b = jnp.exp(m - top)
    top_ref[at] = top
    num_ref[at] = num_ref[at] * a + us[:, :TILE] * b
    den_ref[at] = den_ref[at] * a + us[:, TILE:] * b


def kernel(
    feat_hbm, wsrc_hbm, wdst_hbm, attn_hbm, bias_hbm, mask_hbm, tdst_hbm, tsrc_hbm, count_hbm,
    out_ref,
    feat, wsrc, wdst, attn, bias, mask, attn_sm, tdst, tsrc, tcount, load_sem,
    xg0, xg1, stage, mstage, xs, mk, nu, nuv, own, vt, e_ref, num, den, top, alin, aw, brep,
    floor_ref, lin, table, gsend, grecv, asend, arecv, msend, mrecv,
):
    s = lax.axis_index("src")
    d = lax.axis_index("dst")
    x, zl, core = s // 4, (s // 2) % 2, s % 2
    zh, y = d // 4, d % 4

    def at(xx, zz, cc):
        return lax.rem(xx + 4, 4) * 4 + zz * 2 + cc

    sib = at(x, zl, 1 - core)
    zn = at(x, 1 - zl, core)
    xp = at(x + 1, zl, core)
    xm = at(x - 1, zl, core)
    dest = [lax.rem(zh + r // 4, 2) * 4 + lax.rem(y + r % 4, 4) for r in range(8)]

    loads = []

    def load(src, dst):
        copy = pltpu.make_async_copy(src, dst, load_sem.at[len(loads)])
        copy.start()
        loads.append(copy)

    def columns(ref, k):
        return ref.at[:, pl.ds(k * TILE, TILE)]

    load(feat_hbm, feat)
    for st in range(2):
        for k in range(2):
            load(columns(wsrc_hbm, st + 2 * k), wsrc.at[st, :, pl.ds(k * TILE, TILE)])
    load(tdst_hbm, tdst)
    load(tsrc_hbm, tsrc)
    load(count_hbm, tcount)
    load(mask_hbm, mask)
    for st in range(2):
        for k in range(2):
            load(columns(wdst_hbm, st + 2 * k), wdst.at[st, :, pl.ds(k * TILE, TILE)])
    load(attn_hbm, attn)
    load(attn_hbm, attn_sm)
    load(bias_hbm, bias)

    barrier = pltpu.get_barrier_semaphore()
    partners = [(p, d) for p in (sib, zn, xp, xm)] + [(s, dest[r]) for r in range(1, 8)]
    for partner in partners:
        pl.semaphore_signal(barrier, inc=1, device_id=partner, device_id_type=MESH)

    xg = (xg0, xg1)
    copies = []

    def send(st, slot, part, to):
        ref = xg[st].at[slot] if part is None else xg[st].at[slot, part]
        copy = pltpu.make_async_remote_copy(
            src_ref=ref,
            dst_ref=ref,
            send_sem=gsend.at[len(copies)],
            recv_sem=grecv.at[st, slot, part or 0],
            device_id=(to, d),
            device_id_type=MESH,
        )
        copy.start()
        copies.append(copy)

    def arrived(st, slot, part=None):
        ref = xg[st].at[slot] if part is None else xg[st].at[slot, part]
        pltpu.make_async_remote_copy(
            src_ref=ref,
            dst_ref=ref,
            send_sem=gsend.at[0],
            recv_sem=grecv.at[st, slot, part or 0],
            device_id=(sib, d),
            device_id_type=MESH,
        ).wait_recv()

    def project(st):
        xl = mm(feat[...], wsrc[st]).astype(bf16)
        own[st] = xl
        xg[st][s] = xl.reshape(2, TILE, 256)

    for copy in loads[:3]:
        copy.wait()
    project(0)
    pl.semaphore_wait(barrier, len(partners))
    for to in (zn, xp, xm, sib):
        send(0, s, None, to)
    for copy in loads[3:5]:
        copy.wait()
    project(1)
    send(1, s, None, zn)

    def relay_plane(st):
        arrived(st, zn)
        for to in (xp, xm, sib):
            send(st, zn, None, to)

    def relay_near(st, z):
        left, right = at(x - 1, z, core), at(x + 1, z, core)
        arrived(st, left)
        send(st, left, 0, xp)
        send(st, left, None, sib)
        arrived(st, right)
        send(st, right, 1, xm)
        send(st, right, None, sib)

    def relay_far(st):
        for z in (zl, 1 - zl):
            for part in range(2):
                arrived(st, at(x + 2, z, core), part)
                send(st, at(x + 2, z, core), part, sib)

    def siblings(st):
        for z in (zl, 1 - zl):
            for dx in (0, 1, -1):
                arrived(st, at(x + dx, z, 1 - core))
        for z in (zl, 1 - zl):
            for part in range(2):
                arrived(st, at(x + 2, z, 1 - core), part)

    tile_copies = {}

    def exchange(st):
        for k in range(2):
            for r in (4, 6, 5, 7, 2, 1, 3, 0):
                src = table[0, dest[r] * 2 + k]
                tile = xg[st][src // 2, src % 2]
                if r == 0:
                    xs[st, k] = tile
                    continue
                stage[st, r * 2 + k] = tile
                copy = pltpu.make_async_remote_copy(
                    src_ref=stage.at[st, r * 2 + k],
                    dst_ref=xs.at[st, r * 2 + k],
                    send_sem=asend.at[st, k, r],
                    recv_sem=arecv.at[st, k, r],
                    device_id=(s, dest[r]),
                    device_id_type=MESH,
                )
                copy.start()
                tile_copies[st, k, r] = copy

    def project_dst(st):
        nu[st] = -mm(feat[...], wdst[st]).astype(bf16).astype(f32)

    relay_plane(0)
    relay_near(0, zl)
    for copy in loads[9:]:
        copy.wait()
    relay_near(0, 1 - zl)
    for to in (xp, xm, sib):
        send(1, s, None, to)
    relay_plane(1)

    for copy in loads[5:9]:
        copy.wait()

    def fill(t_dst, _):
        src, slot, used = jnp.int32(0), jnp.int32(0), jnp.int32(0)
        for t in range(16):
            hit = jnp.where((tdst[t] == t_dst) & (t < tcount[0, 0]), 1, 0)
            src, slot, used = src + hit * tsrc[t], slot + hit * t, used + hit
        table[0, t_dst] = src
        table[1, t_dst] = slot
        table[2, t_dst] = used
        return 0

    lax.fori_loop(0, 16, fill, 0)
    mask_copies = []
    for r in range(8):
        for k in range(2):
            tile = dest[r] * 2 + k
            words = mask[table[1, tile]] * table[2, tile]
            if r == 0:
                mk[k] = words
            else:
                mstage[r * 2 + k] = words
        if r:
            copy = pltpu.make_async_remote_copy(
                src_ref=mstage.at[pl.ds(r * 2, 2)],
                dst_ref=mk.at[pl.ds(r * 2, 2)],
                send_sem=msend.at[r],
                recv_sem=mrecv.at[r],
                device_id=(s, dest[r]),
                device_id_type=MESH,
            )
            copy.start()
            mask_copies.append(copy)

    relay_far(0)
    siblings(0)
    exchange(0)
    project_dst(0)
    relay_near(1, zl)
    project_dst(1)
    relay_near(1, 1 - zl)
    make_coefficients(attn, alin, aw, brep)
    for st in range(2):
        prepare_self(st, nu, own, brep, num, den, top)
    for copy in mask_copies:
        copy.wait_recv()

    def floors(u, _):
        floor_ref[u] = mask_bias(mk[u])
        return 0

    lax.fori_loop(0, 16, floors, 0, unroll=2)
    relay_far(1)

    def begin(st, dtile):
        for r in range(1, 8):
            tile_copies[st, dtile, r].wait_recv()
        if dtile == 0:
            for h2 in range(2):
                part = nu[st, :, :TILE]
                nuv[h2] = part if h2 == 0 else pltpu.roll(part, 64, 1)

        def turn(g, _):
            u = 2 * g + dtile
            vt[u] = xs[st, u, :, :TILE].astype(f32).T
            res = nt(alin[st], xs[st, u])
            lin[st, u] = res[:8] + res[8:]
            return 0

        lax.fori_loop(0, 8, turn, 0, unroll=4)

    for st in range(2):
        for dtile in range(2):
            if (st, dtile) == (0, 1):
                siblings(1)
                exchange(1)
            begin(st, dtile)

            def step(n, _):
                logits_step(st, dtile, n, nuv, nu, xs, vt, attn_sm, aw, e_ref)
                return 0

            def finish(n, _):
                finish_step(st, dtile, n, xs, floor_ref, lin, e_ref, num, den, top)
                return 0

            lax.fori_loop(0, 16, step, 0, unroll=2)
            lax.fori_loop(0, 16, finish, 0, unroll=8)

    for st in range(2):
        for k in range(2):
            q = 2 * st + k
            ls = slice((st + 2 * k) * TILE, (st + 2 * k + 1) * TILE)
            out_ref[:, ls] = (num[q] / den[q] + bias[:, ls]).astype(bf16)
    for copy in copies + mask_copies + list(tile_copies.values()):
        copy.wait_send()


def body(features, w_src, w_dst, attn, bias, tile_masks, tile_dst, tile_src, tile_count):
    hbm = pl.BlockSpec(memory_space=pl.ANY)
    dma = pltpu.SemaphoreType.DMA
    scratch = [
        pltpu.VMEM((256, 1024), bf16),
        pltpu.VMEM((2, 1024, 256), bf16),
        pltpu.VMEM((2, 1024, 256), bf16),
        pltpu.VMEM((8, 64), f32),
        pltpu.VMEM((1, 512), f32),
        pltpu.VMEM((16, 8, TILE), i32),
        pltpu.SMEM((8, 64), f32),
        pltpu.SMEM((16,), i32),
        pltpu.SMEM((16,), i32),
        pltpu.SMEM((1, 1), i32),
        dma((16,)),
        pltpu.VMEM((16, 2, TILE, 256), bf16),
        pltpu.VMEM((16, 2, TILE, 256), bf16),
        pltpu.VMEM((2, 16, TILE, 256), bf16),
        pltpu.VMEM((16, 8, TILE), i32),
        pltpu.VMEM((2, 16, TILE, 256), bf16),
        pltpu.VMEM((16, 8, TILE), i32),
        pltpu.VMEM((2, 256, 256), f32),
        pltpu.VMEM((2, 256, TILE), f32),
        pltpu.VMEM((2, 256, 256), bf16),
        pltpu.VMEM((16, TILE, TILE), f32),
        pltpu.VMEM((8, 2, 256, TILE), f32),
        pltpu.VMEM((4, 256, TILE), f32),
        pltpu.VMEM((4, 256, TILE), f32),
        pltpu.VMEM((4, 256, TILE), f32),
        pltpu.VMEM((2, 16, 256), bf16),
        pltpu.VMEM((2, 16, 256), bf16),
        pltpu.VMEM((4, TILE, 512), bf16),
        pltpu.VMEM((16, TILE, TILE), f32),
        pltpu.VMEM((2, 16, 8, TILE), f32),
        pltpu.SMEM((3, 16), i32),
        dma((38,)),
        dma((2, 16, 2)),
        dma((2, 2, 8)),
        dma((2, 2, 8)),
        dma((8,)),
        dma((8,)),
    ]
    return pl.pallas_call(
        kernel,
        out_shape=jax.ShapeDtypeStruct((256, 512), bf16),
        in_specs=[hbm] * 9,
        out_specs=pl.BlockSpec(memory_space=pltpu.VMEM),
        scratch_shapes=scratch,
        compiler_params=pltpu.CompilerParams(
            collective_id=0, has_side_effects=True, vmem_limit_bytes=60 * 2**20
        ),
    )(
        features, w_src, w_dst, attn, bias.reshape(1, 512), tile_masks[0, 0],
        tile_dst[0, 0], tile_src[0, 0], tile_count,
    )


def solution(mesh):
    return jax.shard_map(
        body,
        mesh=mesh,
        in_specs=(
            P(("src", "dst"), None),
            P(),
            P(),
            P(),
            P(),
            P("src", "dst", None, None, None),
            P("src", "dst", None),
            P("src", "dst", None),
            P("src", "dst"),
        ),
        out_specs=P(("src", "dst"), None),
        check_vma=False,
    )
```

```python
import functools

import jax
import jax.numpy as jnp
from jax import lax
from jax.experimental import pallas as pl
from jax.experimental.pallas import tpu as pltpu
from jax.sharding import PartitionSpec as P

f32, bf16, i32 = jnp.float32, jnp.bfloat16, jnp.int32
MESH = pl.DeviceIdType.MESH
TILE = 128
FLOOR = -1e30
HALF_FLOOR = -5e29


def nt(a, b):
    return lax.dot_general(a, b, (((1,), (1,)), ((), ())), preferred_element_type=f32)


def mm(a, b):
    return jnp.dot(a, b, preferred_element_type=f32)


def split(x):
    hi = x.astype(bf16)
    return hi, (x - hi.astype(f32)).astype(bf16)


def iota(shape, dim):
    return lax.broadcasted_iota(i32, shape, dim)


def make_coefficients(attn_ref, alin_ref, aw_ref, brep_ref):
    attn = attn_ref[...]
    tiled = jnp.concatenate([attn] * 8, 1)
    diag = jnp.where(iota((8, 512), 0) == iota((8, 512), 1) // 64, tiled, 0.0)
    flat = jnp.sum(diag, axis=0, keepdims=True)
    same = iota((TILE, TILE), 0) // 64 == iota((TILE, TILE), 1) // 64
    for hp in range(4):
        row = jnp.broadcast_to(flat[:, hp * TILE : (hp + 1) * TILE], (TILE, TILE))
        rep = jnp.where(same, row.T, 0.0)
        parts = split(rep) + split(-0.8 * rep)
        for k, part in enumerate(parts):
            brep_ref[hp, :, k * TILE : (k + 1) * TILE] = part
    k4 = iota((8, TILE), 0) % 4
    half = iota((8, TILE), 1) // 64
    for st in range(2):
        fv = jnp.broadcast_to(flat[:, st * TILE : (st + 1) * TILE], (8, TILE))
        fw = jnp.broadcast_to(flat[:, (st + 2) * TILE : (st + 3) * TILE], (8, TILE))
        lin = jnp.concatenate(
            [jnp.where(k4 == half, fv, 0.0), jnp.where(k4 - 2 == half, fw, 0.0)], 1
        )
        hi, lo = split(lin)
        alin_ref[st] = jnp.concatenate([hi, lo], 0)
        both = -0.8 * jnp.concatenate(
            [jnp.where(k4 == half, fw, 0.0), jnp.where(k4 - 2 == half, fw, 0.0)], 1
        )
        hi, lo = split(both)
        aw_ref[st] = jnp.concatenate([hi, lo], 0)


def prepare_self(st, nu_ref, own_ref, brep_ref, num_ref, den_ref, top_ref):
    for k in range(2):
        ls = slice(k * TILE, (k + 1) * TILE)
        v = own_ref[st, :, ls]
        w = jnp.minimum(nu_ref[st, :, ls].astype(bf16), v)
        b = brep_ref[st + 2 * k]
        top_ref[2 * st + k] = (
            mm(v, b[:, :128]) + mm(v, b[:, 128:256]) + mm(w, b[:, 256:384]) + mm(w, b[:, 384:])
        )
        num_ref[2 * st + k] = v.astype(f32)
        den_ref[2 * st + k] = jnp.ones((256, TILE), f32)


def logits_step(st, dtile, step, nuv_ref, nu_ref, xs_ref, vt_ref, attn_sm, aw_ref, e_ref):
    block = step // 2
    h2 = step % 2
    i0 = pl.multiple_of(dtile * TILE + block * 16, 16)
    ublk = nuv_ref[h2, pl.ds(i0, 16), :]
    i8 = pl.multiple_of(dtile * TILE + block * 16 + h2 * 8, 8)
    rows8 = nu_ref[st, pl.ds(i8, 8), TILE:]
    aw = aw_ref[st]
    low = iota((8, TILE), 0) < 4

    def matrix_piece(quad, g):
        xsw = xs_ref[st, 2 * g + dtile, :, TILE:]
        halves = []
        for a in range(2):
            parts = []
            for b in range(2):
                r = quad * 4 + a * 2 + b
                rb = jnp.broadcast_to(rows8[r : r + 1], (16, TILE)).astype(bf16)
                parts.append(jnp.minimum(jnp.tile(rb, (8, 1)), xsw))
            halves.append(jnp.concatenate(parts, 1))
        res = nt(aw, jnp.concatenate(halves, 0))
        res = res[:8] + res[8:16]
        at = pl.multiple_of(block * 32 + h2 * 16 + quad * 8, 8)
        e_ref[g, 1, pl.ds(at, 8), :] = jnp.where(low, res[:, :TILE], res[:, TILE:])
        tokens.append(res[:, :TILE] * 0.0)

    pieces = [(q, g) for q in range(2) for g in range(8)]
    done = 0
    tokens = []
    acc = [jnp.zeros((16, TILE), f32) for _ in range(8)]
    for c in range(64):
        ub = jnp.broadcast_to(ublk[:, c : c + 1], (16, TILE))
        k = c // 4 - 1
        if c % 4 == 0 and 0 <= k < len(tokens):
            ub = ub + jnp.concatenate([tokens[k]] * 2, 0)
        co = attn_sm[st * 2 + h2, c]
        for g in range(8):
            vb = vt_ref[2 * g + dtile, pl.ds(h2 * 64 + c, 1), :]
            acc[g] = acc[g] + co * jnp.minimum(ub, vb)
        while done < len(pieces) and c >= 4 * done - 12:
            matrix_piece(*pieces[done])
            done += 1
    for g in range(8):
        e_ref[g, 0, pl.ds(block * 32 + h2, 16, stride=2), :] = -0.8 * acc[g]


def mask_bias(words):
    parts = jnp.concatenate([words & 255, (words >> 8) & 255], 0).astype(f32).astype(bf16)
    k = iota((16, TILE), 0)
    pick = ((k % 8) * 2 + k // 8 == iota((16, TILE), 1) // 8).astype(f32).astype(bf16)
    spread = lax.dot_general(parts, pick, (((0,), (0,)), ((), ())), preferred_element_type=f32)
    bits = spread.astype(i32) & (1 << (iota((TILE, TILE), 1) % 8))
    return jnp.where(bits != 0, 0.0, FLOOR)


def finish_step(st, dtile, step, xs_ref, floor_ref, lin_ref, e_ref, num_ref, den_ref, top_ref):
    g = step // 2
    pair = step % 2
    u = 2 * g + dtile
    even = iota((TILE, TILE), 1) < 64
    evenb = even.astype(f32).astype(bf16)
    oddb = (1 - even.astype(f32)).astype(bf16)
    bias = floor_ref[u]
    ps, ms = [], []
    for h2 in range(2):
        e = e_ref[g, pair, pl.ds(h2, TILE, stride=2), :]
        s = e + (lin_ref[st, u, pl.ds(pair * 2 + h2, 1), :] + bias)
        m = jnp.max(s, axis=1, keepdims=True)
        ps.append(jnp.exp(s - jnp.maximum(m, HALF_FLOOR)).astype(bf16))
        ms.append(m)
    p = jnp.concatenate(ps, 1)
    xp = xs_ref[st, u, :, pl.ds(pl.multiple_of(pair * TILE, TILE), TILE)]
    wt = jnp.concatenate(
        [jnp.concatenate([xp * evenb, evenb], 1), jnp.concatenate([xp * oddb, oddb], 1)], 0
    )
    us = mm(p, wt)
    m = jnp.where(even, ms[0], ms[1])
    at = (2 * st + pair, pl.ds(pl.multiple_of(dtile * TILE, TILE), TILE), slice(None))
    old = top_ref[at]
    top = jnp.maximum(old, m)
    a = jnp.exp(old - top)
    b = jnp.exp(m - top)
    top_ref[at] = top
    num_ref[at] = num_ref[at] * a + us[:, :TILE] * b
    den_ref[at] = den_ref[at] * a + us[:, TILE:] * b


def kernel(
    feat_hbm, wsrc_hbm, wdst_hbm, attn_hbm, bias_hbm, mask_hbm, tdst_hbm, tsrc_hbm, count_hbm,
    out_ref,
    feat, wsrc, wdst, attn, bias, mask, attn_sm, tdst, tsrc, tcount, load_sem,
    xg0, xg1, stage, mstage, xs, mk, nu, nuv, own, vt, e_ref, num, den, top, alin, aw, brep,
    floor_ref, lin, table, gsend, grecv, asend, arecv, msend, mrecv,
):
    s = lax.axis_index("src")
    d = lax.axis_index("dst")
    x, zl, core = s // 4, (s // 2) % 2, s % 2
    zh, y = d // 4, d % 4

    def at(xx, zz, cc):
        return lax.rem(xx + 4, 4) * 4 + zz * 2 + cc

    sib = at(x, zl, 1 - core)
    zn = at(x, 1 - zl, core)
    xp = at(x + 1, zl, core)
    xm = at(x - 1, zl, core)
    dest = [lax.rem(zh + r // 4, 2) * 4 + lax.rem(y + r % 4, 4) for r in range(8)]

    loads = []

    def load(src, dst):
        copy = pltpu.make_async_copy(src, dst, load_sem.at[len(loads)])
        copy.start()
        loads.append(copy)

    def columns(ref, k):
        return ref.at[:, pl.ds(k * TILE, TILE)]

    load(feat_hbm, feat)
    for st in range(2):
        for k in range(2):
            load(columns(wsrc_hbm, st + 2 * k), wsrc.at[st, :, pl.ds(k * TILE, TILE)])
    load(tdst_hbm, tdst)
    load(tsrc_hbm, tsrc)
    load(count_hbm, tcount)
    load(mask_hbm, mask)
    for st in range(2):
        for k in range(2):
            load(columns(wdst_hbm, st + 2 * k), wdst.at[st, :, pl.ds(k * TILE, TILE)])
    load(attn_hbm, attn)
    load(attn_hbm, attn_sm)
    load(bias_hbm, bias)

    barrier = pltpu.get_barrier_semaphore()
    partners = [(p, d) for p in (sib, zn, xp, xm)] + [(s, dest[r]) for r in range(1, 8)]
    for partner in partners:
        pl.semaphore_signal(barrier, inc=1, device_id=partner, device_id_type=MESH)

    xg = (xg0, xg1)
    copies = []

    def send(st, slot, part, to):
        ref = xg[st].at[slot] if part is None else xg[st].at[slot, part]
        copy = pltpu.make_async_remote_copy(
            src_ref=ref,
            dst_ref=ref,
            send_sem=gsend.at[len(copies)],
            recv_sem=grecv.at[st, slot, part or 0],
            device_id=(to, d),
            device_id_type=MESH,
        )
        copy.start()
        copies.append(copy)

    def arrived(st, slot, part=None):
        ref = xg[st].at[slot] if part is None else xg[st].at[slot, part]
        pltpu.make_async_remote_copy(
            src_ref=ref,
            dst_ref=ref,
            send_sem=gsend.at[0],
            recv_sem=grecv.at[st, slot, part or 0],
            device_id=(sib, d),
            device_id_type=MESH,
        ).wait_recv()

    def project(st):
        xl = mm(feat[...], wsrc[st]).astype(bf16)
        own[st] = xl
        xg[st][s] = xl.reshape(2, TILE, 256)

    for copy in loads[:3]:
        copy.wait()
    project(0)
    pl.semaphore_wait(barrier, len(partners))
    for to in (zn, xp, xm, sib):
        send(0, s, None, to)
    for copy in loads[3:5]:
        copy.wait()
    project(1)
    send(1, s, None, zn)

    def relay_plane(st):
        arrived(st, zn)
        for to in (xp, xm, sib):
            send(st, zn, None, to)

    def relay_near(st, z):
        left, right = at(x - 1, z, core), at(x + 1, z, core)
        arrived(st, left)
        send(st, left, 0, xp)
        send(st, left, None, sib)
        arrived(st, right)
        send(st, right, 1, xm)
        send(st, right, None, sib)

    def relay_far(st):
        for z in (zl, 1 - zl):
            for part in range(2):
                arrived(st, at(x + 2, z, core), part)
                send(st, at(x + 2, z, core), part, sib)

    def siblings(st):
        for z in (zl, 1 - zl):
            for dx in (0, 1, -1):
                arrived(st, at(x + dx, z, 1 - core))
        for z in (zl, 1 - zl):
            for part in range(2):
                arrived(st, at(x + 2, z, 1 - core), part)

    tile_copies = {}

    def exchange(st):
        for k in range(2):
            for r in (4, 6, 5, 7, 2, 1, 3, 0):
                src = table[0, dest[r] * 2 + k]
                tile = xg[st][src // 2, src % 2]
                if r == 0:
                    xs[st, k] = tile
                    continue
                stage[st, r * 2 + k] = tile
                copy = pltpu.make_async_remote_copy(
                    src_ref=stage.at[st, r * 2 + k],
                    dst_ref=xs.at[st, r * 2 + k],
                    send_sem=asend.at[st, k, r],
                    recv_sem=arecv.at[st, k, r],
                    device_id=(s, dest[r]),
                    device_id_type=MESH,
                )
                copy.start()
                tile_copies[st, k, r] = copy

    def project_dst(st):
        nu[st] = -mm(feat[...], wdst[st]).astype(bf16).astype(f32)

    relay_plane(0)
    relay_near(0, zl)
    for copy in loads[9:]:
        copy.wait()
    relay_near(0, 1 - zl)
    for to in (xp, xm, sib):
        send(1, s, None, to)
    relay_plane(1)

    for copy in loads[5:9]:
        copy.wait()

    def fill(t_dst, _):
        src, slot, used = jnp.int32(0), jnp.int32(0), jnp.int32(0)
        for t in range(16):
            hit = jnp.where((tdst[t] == t_dst) & (t < tcount[0, 0]), 1, 0)
            src, slot, used = src + hit * tsrc[t], slot + hit * t, used + hit
        table[0, t_dst] = src
        table[1, t_dst] = slot
        table[2, t_dst] = used
        return 0

    lax.fori_loop(0, 16, fill, 0)
    mask_copies = []
    for r in range(8):
        for k in range(2):
            tile = dest[r] * 2 + k
            words = mask[table[1, tile]] * table[2, tile]
            if r == 0:
                mk[k] = words
            else:
                mstage[r * 2 + k] = words
        if r:
            copy = pltpu.make_async_remote_copy(
                src_ref=mstage.at[pl.ds(r * 2, 2)],
                dst_ref=mk.at[pl.ds(r * 2, 2)],
                send_sem=msend.at[r],
                recv_sem=mrecv.at[r],
                device_id=(s, dest[r]),
                device_id_type=MESH,
            )
            copy.start()
            mask_copies.append(copy)

    relay_far(0)
    siblings(0)
    exchange(0)
    project_dst(0)
    relay_near(1, zl)
    project_dst(1)
    relay_near(1, 1 - zl)
    make_coefficients(attn, alin, aw, brep)
    for st in range(2):
        prepare_self(st, nu, own, brep, num, den, top)
    for copy in mask_copies:
        copy.wait_recv()

    def floors(u, _):
        floor_ref[u] = mask_bias(mk[u])
        return 0

    lax.fori_loop(0, 16, floors, 0, unroll=2)
    relay_far(1)

    def begin(st, dtile):
        for r in range(1, 8):
            tile_copies[st, dtile, r].wait_recv()
        if dtile == 0:
            for h2 in range(2):
                part = nu[st, :, :TILE]
                nuv[h2] = part if h2 == 0 else pltpu.roll(part, 64, 1)

        def turn(g, _):
            u = 2 * g + dtile
            vt[u] = xs[st, u, :, :TILE].astype(f32).T
            res = nt(alin[st], xs[st, u])
            lin[st, u] = res[:8] + res[8:]
            return 0

        lax.fori_loop(0, 8, turn, 0, unroll=4)

    for st in range(2):
        for dtile in range(2):
            if (st, dtile) == (0, 1):
                siblings(1)
                exchange(1)
            begin(st, dtile)

            def step(n, _):
                logits_step(st, dtile, n, nuv, nu, xs, vt, attn_sm, aw, e_ref)
                return 0

            def finish(n, _):
                finish_step(st, dtile, n, xs, floor_ref, lin, e_ref, num, den, top)
                return 0

            lax.fori_loop(0, 16, step, 0, unroll=2)
            lax.fori_loop(0, 16, finish, 0, unroll=8)

    for st in range(2):
        for k in range(2):
            q = 2 * st + k
            ls = slice((st + 2 * k) * TILE, (st + 2 * k + 1) * TILE)
            out_ref[:, ls] = (num[q] / den[q] + bias[:, ls]).astype(bf16)
    for copy in copies + mask_copies + list(tile_copies.values()):
        copy.wait_send()


def body(features, w_src, w_dst, attn, bias, tile_masks, tile_dst, tile_src, tile_count):
    hbm = pl.BlockSpec(memory_space=pl.ANY)
    dma = pltpu.SemaphoreType.DMA
    scratch = [
        pltpu.VMEM((256, 1024), bf16),
        pltpu.VMEM((2, 1024, 256), bf16),
        pltpu.VMEM((2, 1024, 256), bf16),
        pltpu.VMEM((8, 64), f32),
        pltpu.VMEM((1, 512), f32),
        pltpu.VMEM((16, 8, TILE), i32),
        pltpu.SMEM((8, 64), f32),
        pltpu.SMEM((16,), i32),
        pltpu.SMEM((16,), i32),
        pltpu.SMEM((1, 1), i32),
        dma((16,)),
        pltpu.VMEM((16, 2, TILE, 256), bf16),
        pltpu.VMEM((16, 2, TILE, 256), bf16),
        pltpu.VMEM((2, 16, TILE, 256), bf16),
        pltpu.VMEM((16, 8, TILE), i32),
        pltpu.VMEM((2, 16, TILE, 256), bf16),
        pltpu.VMEM((16, 8, TILE), i32),
        pltpu.VMEM((2, 256, 256), f32),
        pltpu.VMEM((2, 256, TILE), f32),
        pltpu.VMEM((2, 256, 256), bf16),
        pltpu.VMEM((16, TILE, TILE), f32),
        pltpu.VMEM((8, 2, 264, TILE), f32),
        pltpu.VMEM((4, 256, TILE), f32),
        pltpu.VMEM((4, 256, TILE), f32),
        pltpu.VMEM((4, 256, TILE), f32),
        pltpu.VMEM((2, 16, 256), bf16),
        pltpu.VMEM((2, 16, 256), bf16),
        pltpu.VMEM((4, TILE, 512), bf16),
        pltpu.VMEM((16, TILE, TILE), f32),
        pltpu.VMEM((2, 16, 8, TILE), f32),
        pltpu.SMEM((3, 16), i32),
        dma((38,)),
        dma((2, 16, 2)),
        dma((2, 2, 8)),
        dma((2, 2, 8)),
        dma((8,)),
        dma((8,)),
    ]
    return pl.pallas_call(
        kernel,
        out_shape=jax.ShapeDtypeStruct((256, 512), bf16),
        in_specs=[hbm] * 9,
        out_specs=pl.BlockSpec(memory_space=pltpu.VMEM),
        scratch_shapes=scratch,
        compiler_params=pltpu.CompilerParams(
            collective_id=0, has_side_effects=True, vmem_limit_bytes=60 * 2**20
        ),
    )(
        features, w_src, w_dst, attn, bias.reshape(1, 512), tile_masks[0, 0],
        tile_dst[0, 0], tile_src[0, 0], tile_count,
    )


def solution(mesh):
    return jax.shard_map(
        body,
        mesh=mesh,
        in_specs=(
            P(("src", "dst"), None),
            P(),
            P(),
            P(),
            P(),
            P("src", "dst", None, None, None),
            P("src", "dst", None),
            P("src", "dst", None),
            P("src", "dst"),
        ),
        out_specs=P(("src", "dst"), None),
        check_vma=False,
    )
```
